32 devices in a mesh: ctx: 16 (over z, x, core), head: 2 (over y).
Axes of the slice: x: 2, y: 2, z: 4, core: 2. Of those that a mesh axis runs over, the one named last changes fastest.
Arguments:
- tokens: bfloat16 [12288, 1024], P('ctx')
- qkv_weight: bfloat16 [1024, 3, 1024], P('ctx', None, 'head'), may hold values from -0.1875 to 0.1875
- grad_attn: bfloat16 [12288, 1024], P('ctx', 'head'), may hold values from -6 to 6
- positions: int32 [12288], P('ctx'), may hold values from 0 to 786431, as said below
- slopes: float32 [16], P('head'), may hold values from 0.03 to 0.6
Outputs:
- d_tokens: bfloat16 [12288, 1024], P('ctx')
- d_weight: float32 [1024, 3, 1024], P('ctx', None, 'head')
The draws below stay inside these ranges and needn't reach their ends.
Inputs may be any that keep to these rules, and one draw needn't show every extreme that they name: positions rise strictly along the sequence, start at 0 and end at 786431; neighbours differ by 1 to 127.
All inputs are finite; a program needn't handle non-finite values.
Results may differ from the reference program's by a relative error of at most 0.006.
The reference program's roundings to bfloat16 on the way count: a program that leaves them out, or rounds other values in their place, can miss the bound.
Values may be sent and summed in bfloat16 or wider, within the bound.
A program may use at most 128 MiB of HBM per device.

```python
import math
import jax
import jax.numpy as jnp
from jax import lax

D = 1024
H = 16
HD = 64
ROWS = 768
TOKENS = 12288


def draw_tokens(key, part):
    key = jax.random.fold_in(key, 11)
    first = jax.random.fold_in(key, 0)
    third = jax.random.fold_in(key, 2)
    blocks = TOKENS // ROWS
    base = jax.random.normal(first, (TOKENS, D), jnp.float32)
    pairing = jax.random.permutation(third, blocks)
    width = D // blocks
    row_block = jnp.arange(TOKENS, dtype=jnp.int32) // ROWS
    col_block = jnp.arange(D, dtype=jnp.int32) // width
    spike = jnp.where(pairing[row_block][:, None] == col_block[None, :], 3.0, 1.0).astype(jnp.float32)
    return (base * spike).astype(jnp.bfloat16)


def draw_positions(key, part):
    key = jax.random.fold_in(key, 23)
    extra = jax.random.randint(key, (TOKENS,), 0, 64, dtype=jnp.int32)
    index = jnp.arange(TOKENS, dtype=jnp.int32)
    extra = jnp.where(index == 0, 0, extra)
    extra = jnp.where(index == TOKENS - 1, 63, extra)
    return (64 * index + extra).astype(jnp.int32)


def block_levels(rng, shape, cuts, smallest, high):
    def one(position, shards_of):
        heights = jax.random.uniform(jax.random.fold_in(jax.random.fold_in(rng, 6), position), (shards_of,), jnp.float32, smallest / len(cuts), high / len(cuts))
        return jnp.repeat(jnp.exp(heights), shape[position] // shards_of).reshape((-1,) + (1,) * (len(shape) - position - 1))

    gain = one(*cuts[0])
    for cut in cuts[1:]:
        gain = gain * one(*cut)
    return gain


def gaussian(key, dims, scale, most, cuts=(), held_as=jnp.bfloat16):
    values = scale * jax.random.normal(key, dims, jnp.float32)
    if cuts:
        values = values * block_levels(key, dims, cuts, -0.22, 0.18)
    return jnp.clip(values, -most, most).astype(held_as)


def setup_inputs(seed: int = 0) -> dict:
    splits = jax.random.split(jax.random.key(seed), 6)
    return {
        "tokens": draw_tokens(jax.random.fold_in(splits[5], 71), 0),
        "qkv_weight": gaussian(splits[1], (D, 3, D), D ** -0.5, 0.1875, ((0, 16), (2, 2))),
        "grad_attn": gaussian(splits[2], (TOKENS, D), 1.0, 6.0, ((0, 16), (1, 2))),
        "positions": draw_positions(jax.random.fold_in(splits[5], 71), 0),
        "slopes": jnp.clip(jnp.exp(math.log(0.6) - 2.9957323 * jax.random.uniform(splits[4], (H,), jnp.float32) ** block_levels(splits[4], (H,), ((0, 2),), -0.2, 0.2)), 0.03, 0.6),
    }


def block_grads(q, k, v, grad_heads, positions, slopes, block):
    half = (TOKENS // ROWS) // 2
    far = jnp.bitwise_xor(block, half).astype(jnp.int32)
    start = (block * ROWS).astype(jnp.int32)
    far_start = (far * ROWS).astype(jnp.int32)
    q_blk = lax.dynamic_slice_in_dim(q, start, ROWS, 0).astype(jnp.float32)
    g_blk = lax.dynamic_slice_in_dim(grad_heads, start, ROWS, 0).astype(jnp.float32)
    k_all = jnp.concatenate([lax.dynamic_slice_in_dim(k, start, ROWS, 0), lax.dynamic_slice_in_dim(k, far_start, ROWS, 0)], 0).astype(jnp.float32)
    v_all = jnp.concatenate([lax.dynamic_slice_in_dim(v, start, ROWS, 0), lax.dynamic_slice_in_dim(v, far_start, ROWS, 0)], 0).astype(jnp.float32)
    pos_q = lax.dynamic_slice_in_dim(positions, start, ROWS, 0)
    pos_all = jnp.concatenate([pos_q, lax.dynamic_slice_in_dim(positions, far_start, ROWS, 0)], 0)
    logd = jnp.log1p(jnp.abs(pos_q[:, None] - pos_all[None, :]).astype(jnp.float32))
    scale = HD ** -0.5
    score = jnp.einsum("qhe,khe->hqk", q_blk, k_all) * scale - slopes[:, None, None] * logd[None]
    top = jnp.max(score, axis=-1, keepdims=True)
    expd = jnp.exp(score - top)
    prob = expd / jnp.sum(expd, axis=-1, keepdims=True)
    prob_round = prob.astype(jnp.bfloat16).astype(jnp.float32)
    outv = jnp.einsum("hqk,khe->qhe", prob_round, v_all)
    delta = jnp.sum(g_blk * outv, axis=-1)
    delta = jnp.transpose(delta)[:, :, None]
    dprob = jnp.einsum("qhe,khe->hqk", g_blk, v_all)
    dscore = (prob * (dprob - delta) * scale).astype(jnp.bfloat16).astype(jnp.float32)
    dq = jnp.einsum("hqk,khe->qhe", dscore, k_all)
    dk = jnp.einsum("hqk,qhe->khe", dscore, q_blk)
    dv = jnp.einsum("hqk,qhe->khe", prob_round, g_blk)
    return dq, dk, dv


def reference(tokens, qkv_weight, grad_attn, positions, slopes):
    nblocks = TOKENS // ROWS
    qkv = jnp.einsum("sd,dcf->scf", tokens.astype(jnp.float32), qkv_weight.astype(jnp.float32)).astype(jnp.bfloat16)
    q = qkv[:, 0].reshape(TOKENS, H, HD)
    k = qkv[:, 1].reshape(TOKENS, H, HD)
    v = qkv[:, 2].reshape(TOKENS, H, HD)
    grad_heads = grad_attn.reshape(TOKENS, H, HD)

    def one_block(block):
        return block_grads(q, k, v, grad_heads, positions, slopes, block)

    dq, dk_all, dv_all = lax.map(one_block, jnp.arange(nblocks, dtype=jnp.int32))
    paired = jnp.bitwise_xor(jnp.arange(nblocks, dtype=jnp.int32), nblocks // 2)
    dk = dk_all[:, :ROWS] + dk_all[paired, ROWS:]
    dv = dv_all[:, :ROWS] + dv_all[paired, ROWS:]
    dqkv = jnp.stack([dq.reshape(TOKENS, D).astype(jnp.bfloat16), dk.reshape(TOKENS, D).astype(jnp.bfloat16), dv.reshape(TOKENS, D).astype(jnp.bfloat16)], 1)
    dqkv_wide = dqkv.astype(jnp.float32)
    d_tokens = jnp.einsum("scf,dcf->sd", dqkv_wide, qkv_weight.astype(jnp.float32)).astype(jnp.bfloat16)
    d_weight = jnp.einsum("sd,scf->dcf", tokens.astype(jnp.float32), dqkv_wide)
    return d_tokens, d_weight
```

```python
import functools
import math

import jax
import jax.numpy as jnp
from jax import lax
from jax.experimental import pallas as pl
from jax.experimental.pallas import tpu as pltpu
from jax.sharding import PartitionSpec as P

F32 = jnp.float32
BF16 = jnp.bfloat16
LOG2E = math.log2(math.e)
PAIR = 128
TILE = 256


def flip(value, axis, mask):
    pairs = [(source, source ^ mask) for source in range(lax.axis_size(axis))]
    return lax.ppermute(value, axis, pairs)


def ordered(mine, other, bit):
    first = jnp.concatenate([mine, other], 0)
    second = jnp.concatenate([other, mine], 0)
    return jnp.where(bit == 0, first, second)


def attention_kernel(slope_ref, q_ref, k_ref, kt_ref, v_ref, g_ref, logd_ref, own_ref, far_ref, dk_acc, dv_acc):
    step = pl.program_id(0)
    steps = pl.num_programs(0)
    half = steps // 2
    size = PAIR // 2
    rows = own_ref.shape[1]
    scale = size ** (-0.5)

    @pl.when(step == 0)
    def _():
        dk_acc[...] = jnp.zeros_like(dk_acc)
        dv_acc[...] = jnp.zeros_like(dv_acc)

    lane = lax.broadcasted_iota(jnp.int32, (TILE, PAIR), 1)
    key = k_ref[...]
    key_t = kt_ref[...]
    value = v_ref[...]
    query = q_ref[...].astype(F32)
    grad = g_ref[...].astype(F32)
    contract_last = (((1,), (1,)), ((), ()))
    grads_q = []
    for head in range(2):
        here = (lane >= head * size) & (lane < (head + 1) * size)
        q_head = jnp.where(here, query, 0.0).astype(BF16)
        g_head = jnp.where(here, grad, 0.0)
        g_scaled = (g_head * scale).astype(BF16)
        g_head = g_head.astype(BF16)
        score = lax.dot_general(key, q_head, contract_last, preferred_element_type=F32)
        score = score * (scale * LOG2E) - logd_ref[...] * slope_ref[head]
        top = jnp.max(score, axis=0, keepdims=True)
        expd = jnp.exp2(score - top)
        inverse = 1.0 / jnp.sum(expd, axis=0, keepdims=True)
        prob = expd * inverse
        prob_round = prob.astype(BF16)
        dprob = lax.dot_general(value, g_scaled, contract_last, preferred_element_type=F32)
        delta = jnp.sum(prob_round.astype(F32) * dprob, axis=0, keepdims=True)
        dscore = (prob * (dprob - delta)).astype(BF16)
        dv_acc[...] += jnp.dot(prob_round, g_head, preferred_element_type=F32)
        dk_acc[...] += jnp.dot(dscore, q_head, preferred_element_type=F32)
        grad_q = jnp.dot(key_t, dscore, preferred_element_type=F32)
        grads_q.append(grad_q[head * size : (head + 1) * size])
    grad_q = jnp.concatenate(grads_q, 0).T.astype(BF16)

    @pl.when(step < half)
    def _():
        own_ref[0, pl.ds(pl.multiple_of(step * TILE, TILE), TILE), :] = grad_q

    @pl.when(step >= half)
    def _():
        far_ref[0, pl.ds(pl.multiple_of((step - half) * TILE, TILE), TILE), :] = grad_q

    @pl.when(step == steps - 1)
    def _():
        own_ref[1] = dk_acc[:rows].astype(BF16)
        own_ref[2] = dv_acc[:rows].astype(BF16)
        far_ref[1] = dk_acc[rows:].astype(BF16)
        far_ref[2] = dv_acc[rows:].astype(BF16)


def attention(pair, slopes, qkv, keys_t, grad, logd):
    both, width = qkv.shape
    rows = both // 2
    groups = width // (3 * PAIR)
    out = jax.ShapeDtypeStruct((3, rows, PAIR), BF16)
    whole = pl.BlockSpec((3, rows, PAIR), lambda i: (0, 0, 0))
    return pl.pallas_call(
        attention_kernel,
        grid=(both // TILE,),
        out_shape=(out, out),
        in_specs=[
            pl.BlockSpec(memory_space=pltpu.SMEM),
            pl.BlockSpec((TILE, PAIR), lambda i: (i, pair)),
            pl.BlockSpec((both, PAIR), lambda i: (0, groups + pair)),
            pl.BlockSpec((PAIR, both), lambda i: (pair, 0)),
            pl.BlockSpec((both, PAIR), lambda i: (0, 2 * groups + pair)),
            pl.BlockSpec((TILE, PAIR), lambda i: (i, pair)),
            pl.BlockSpec((both, TILE), lambda i: (0, i)),
        ],
        out_specs=(whole, whole),
        scratch_shapes=[pltpu.VMEM((both, PAIR), F32), pltpu.VMEM((both, PAIR), F32)],
        compiler_params=pltpu.CompilerParams(vmem_limit_bytes=48 * 2**20),
        cost_estimate=pl.CostEstimate(
            flops=12 * both * both * PAIR * 2, bytes_accessed=4 * both * both, transcendentals=2 * both * both
        ),
    )(slopes[2 * pair : 2 * pair + 2], qkv, qkv, keys_t, qkv, grad, logd)


def on_device(tokens, qkv_weight, grad_attn, positions, slopes):
    rows, model = tokens.shape
    blocks = lax.axis_size("ctx")
    far_mask = blocks // 2
    bits = far_mask.bit_length() - 1
    me = lax.axis_index("ctx")
    side = me // far_mask
    head_side = lax.axis_index("head")
    shard, _, local_width = qkv_weight.shape
    width = local_width // 2
    heads = slopes.shape[0] // 2
    pairs = width // PAIR
    half_rows = rows // 2

    def bit_of(position):
        return (me // 2**position) % 2

    with jax.named_scope("exchange_inputs"):
        weight_parts = [
            lax.dynamic_slice_in_dim(qkv_weight, which * width, width, 2).reshape(shard, 3 * width)
            for which in (side, 1 - side)
        ]
        far_positions = flip(positions, "ctx", far_mask)
        other_weight = flip(weight_parts[1], "ctx", far_mask)
        token_half = lax.dynamic_slice_in_dim(tokens, head_side * half_rows, half_rows, 0)
        quarter = half_rows // 2
        near, cross = [], []
        for part in range(2):
            arrived = flip(token_half[part * quarter : (part + 1) * quarter], "ctx", far_mask)
            near.append(arrived)
            cross.append(flip(arrived, "head", 1))
        far_tokens = ordered(jnp.concatenate(near, 0), jnp.concatenate(cross, 0), head_side)
        grad_mine = lax.dynamic_slice_in_dim(grad_attn, side * width, width, 1)
        far_grad = flip(lax.dynamic_slice_in_dim(grad_attn, (1 - side) * width, width, 1), "ctx", far_mask)
        grad = jnp.concatenate([grad_mine, far_grad], 0)
        slopes_mine = lax.dynamic_slice_in_dim(slopes, side * heads, heads, 0)

    def gather_weight(mine, other):
        stacked = ordered(mine[None], other[None], side)[:, None]
        for position in reversed(range(bits)):
            arrived = flip(stacked, "ctx", 2**position)
            pieces = (stacked[:, :, None], arrived[:, :, None])
            along = [jnp.concatenate(c, 2) for c in (pieces, pieces[::-1])]
            stacked = jnp.where(bit_of(position) == 0, along[0], along[1])
            stacked = stacked.reshape(2, -1, shard, 3 * width)
        return stacked.reshape(model, 3 * width)

    with jax.named_scope("gather_weight"):
        weight = gather_weight(weight_parts[0], other_weight)

    with jax.named_scope("log_distance"):
        pos = jnp.concatenate([positions, far_positions], 0)
        logd = jnp.log(jnp.abs(pos[:, None] - pos[None, :]).astype(F32) + 1.0) * LOG2E

    with jax.named_scope("project"):
        qkv_own = jnp.dot(tokens, weight, preferred_element_type=F32).astype(BF16)
        qkv_far = jnp.dot(far_tokens, weight, preferred_element_type=F32).astype(BF16)
        qkv = jnp.concatenate([qkv_own, qkv_far], 0)
        keys_t = qkv[:, width : 2 * width].T
        both_tokens = jnp.concatenate([tokens, far_tokens], 0)

    with jax.named_scope("gather_other_weight"):
        late = lax.optimization_barrier((weight_parts[0], weight_parts[1], qkv_own))
        back_weight = flip(late[0], "ctx", far_mask)
        weight_other = gather_weight(late[1], back_weight)

    def reduce_weight(term):
        total = term.reshape(2, far_mask, shard, term.shape[1])
        for position in range(bits):
            bit = bit_of(position)
            folded = total.reshape(2, total.shape[1] // 2, 2, shard, term.shape[1])
            send = lax.dynamic_index_in_dim(folded, 1 - bit, 2, keepdims=False)
            keep = lax.dynamic_index_in_dim(folded, bit, 2, keepdims=False)
            total = keep + flip(send, "ctx", 2**position)
        total = total.reshape(2, shard, term.shape[1])
        keep = lax.dynamic_index_in_dim(total, side, 0, keepdims=False)
        arrived = flip(lax.dynamic_index_in_dim(total, 1 - side, 0, keepdims=False), "ctx", far_mask)
        return keep, arrived

    own, other, terms = [], [], []
    for pair in range(pairs):
        with jax.named_scope("attention"):
            mine, theirs = attention(pair, slopes_mine, qkv, keys_t, grad, logd)
        with jax.named_scope("return_grads"):
            own.append(mine)
            other.append(flip(theirs, "ctx", far_mask))
        with jax.named_scope("weight_grad"):
            stacked = jnp.concatenate([mine, theirs], 1)
            term = jnp.einsum("sd,csf->dcf", both_tokens, stacked, preferred_element_type=F32)
            terms.append(reduce_weight(term.reshape(model, 3 * PAIR)))

    with jax.named_scope("token_grad"):
        dqkv = jnp.concatenate(own + other, 0)
        joined = []
        for array in (weight, weight_other):
            array = array.reshape(model, 3, pairs, PAIR)
            joined.append(array.transpose(2, 1, 0, 3).reshape(3 * pairs, model, PAIR))
        joined = jnp.concatenate(joined, 0)

        def partial_rows(part):
            rows_part = lax.dynamic_slice_in_dim(dqkv, part * half_rows, half_rows, 1)
            return jnp.einsum("csf,cdf->sd", rows_part, joined, preferred_element_type=F32)

        sent = partial_rows(1 - head_side)
        kept = partial_rows(head_side)
        mine, cross = [], []
        for part in range(2):
            cut = slice(part * quarter, (part + 1) * quarter)
            total = (kept[cut] + flip(sent[cut], "head", 1)).astype(BF16)
            mine.append(total)
            cross.append(flip(total, "head", 1))
        d_tokens = ordered(jnp.concatenate(mine, 0), jnp.concatenate(cross, 0), head_side)

    with jax.named_scope("weight_grad_out"):
        keep = jnp.stack([t[0].reshape(shard, 3, PAIR) for t in terms], 2).reshape(shard, 3, width)
        arrived = jnp.stack([t[1].reshape(shard, 3, PAIR) for t in terms], 2).reshape(shard, 3, width)
        d_weight = jnp.where(
            side == 0, jnp.concatenate([keep, arrived], 2), jnp.concatenate([arrived, keep], 2)
        )
    return (d_tokens, d_weight)


def solution(mesh):
    placed = (P("ctx", None), P("ctx", None, "head"), P("ctx", "head"), P("ctx"), P("head"))
    return jax.shard_map(
        on_device,
        mesh=mesh,
        in_specs=placed,
        out_specs=(P("ctx", None), P("ctx", None, "head")),
        check_vma=False,
    )
```

```python
import functools
import math

import jax
import jax.numpy as jnp
from jax import lax
from jax.experimental import pallas as pl
from jax.experimental.pallas import tpu as pltpu
from jax.sharding import PartitionSpec as P

F32 = jnp.float32
BF16 = jnp.bfloat16
LOG2E = math.log2(math.e)
PAIR = 128
TILE = 256


def flip(value, axis, mask):
    pairs = [(source, source ^ mask) for source in range(lax.axis_size(axis))]
    return lax.ppermute(value, axis, pairs)


def ordered(mine, other, bit):
    first = jnp.concatenate([mine, other], 0)
    second = jnp.concatenate([other, mine], 0)
    return jnp.where(bit == 0, first, second)


def attention_kernel(first, deps, *refs):
    slope_ref, q_ref, k_ref, v_ref, g_ref, logd_ref = refs[:6]
    rest = refs[6:]
    if first:
        dq_ref, dk_acc, dv_acc, kt_ref = rest[deps:]
    else:
        far_dq_ref, dk_in, dv_in = rest[:3]
        whole_ref, far_ref, dk_acc, dv_acc, kt_ref = rest[3 + deps :]
    step = pl.program_id(0)
    steps = pl.num_programs(0)
    size = PAIR // 2
    scale = size ** (-0.5)

    @pl.when(step == 0)
    def _():
        kt_ref[...] = k_ref[...].astype(F32).T.astype(BF16)
        if first:
            dk_acc[...] = jnp.zeros_like(dk_acc)
            dv_acc[...] = jnp.zeros_like(dv_acc)
        else:
            dk_acc[...] = dk_in[...]
            dv_acc[...] = dv_in[...]

    lane = lax.broadcasted_iota(jnp.int32, (TILE, PAIR), 1)
    key = k_ref[...]
    key_t = kt_ref[...]
    value = v_ref[...]
    query = q_ref[...].astype(F32)
    grad = g_ref[...].astype(F32)
    contract_last = (((1,), (1,)), ((), ()))
    grads_q = []
    for head in range(2):
        here = (lane >= head * size) & (lane < (head + 1) * size)
        q_head = jnp.where(here, query, 0.0).astype(BF16)
        g_head = jnp.where(here, grad, 0.0)
        g_scaled = (g_head * scale).astype(BF16)
        g_head = g_head.astype(BF16)
        score = lax.dot_general(key, q_head, contract_last, preferred_element_type=F32)
        score = score * (scale * LOG2E) - logd_ref[...] * slope_ref[head]
        top = jnp.max(score, axis=0, keepdims=True)
        expd = jnp.exp2(score - top)
        inverse = 1.0 / jnp.sum(expd, axis=0, keepdims=True)
        prob = expd * inverse
        prob_round = prob.astype(BF16)
        dprob = lax.dot_general(value, g_scaled, contract_last, preferred_element_type=F32)
        delta = jnp.sum(prob_round.astype(F32) * dprob, axis=0, keepdims=True)
        dscore = (prob * (dprob - delta)).astype(BF16)
        dv_acc[...] += jnp.dot(prob_round, g_head, preferred_element_type=F32)
        dk_acc[...] += jnp.dot(dscore, q_head, preferred_element_type=F32)
        grad_q = jnp.dot(key_t, dscore, preferred_element_type=F32)
        grads_q.append(grad_q[head * size : (head + 1) * size])
    grad_q = jnp.concatenate(grads_q, 0).T.astype(BF16)

    if first:
        dq_ref[...] = grad_q
        return

    whole_ref[pl.ds(pl.multiple_of(step * TILE, TILE), TILE), :PAIR] = grad_q

    @pl.when(step == steps - 1)
    def _():
        rows = far_ref.shape[0]
        dk = dk_acc[...].astype(BF16)
        dv = dv_acc[...].astype(BF16)
        whole_ref[rows:, :PAIR] = far_dq_ref[...]
        whole_ref[:, PAIR : 2 * PAIR] = dk
        whole_ref[:, 2 * PAIR :] = dv
        far_ref[:, :PAIR] = dk[rows:]
        far_ref[:, PAIR:] = dv[rows:]


def attention(first, pair, slopes, qkv, grad, logd, earlier, deps):
    both, _ = qkv.shape
    rows = both // 2
    steps = rows // TILE
    start = steps if first else 0
    acc = jax.ShapeDtypeStruct((both, PAIR), F32)
    fixed = lambda *shape: pl.BlockSpec(shape, lambda i: (0, 0))
    out_bf16 = lambda *shape: jax.ShapeDtypeStruct(shape, BF16)
    if first:
        out_shape = (out_bf16(rows, PAIR), acc, acc)
        out_specs = (pl.BlockSpec((TILE, PAIR), lambda i: (i, 0)), fixed(both, PAIR), fixed(both, PAIR))
        scratch = []
        earlier_specs = []
    else:
        out_shape = (out_bf16(both, 3 * PAIR), out_bf16(rows, 2 * PAIR))
        out_specs = (fixed(both, 3 * PAIR), fixed(rows, 2 * PAIR))
        scratch = [pltpu.VMEM((both, PAIR), F32), pltpu.VMEM((both, PAIR), F32)]
        earlier_specs = [fixed(rows, PAIR), fixed(both, PAIR), fixed(both, PAIR)]
    return pl.pallas_call(
        functools.partial(attention_kernel, first, len(deps)),
        grid=(steps,),
        out_shape=out_shape,
        in_specs=[
            pl.BlockSpec(memory_space=pltpu.SMEM),
            pl.BlockSpec((TILE, PAIR), lambda i: (start + i, 3 * pair)),
            pl.BlockSpec((both, PAIR), lambda i: (0, 3 * pair + 1)),
            pl.BlockSpec((both, PAIR), lambda i: (0, 3 * pair + 2)),
            pl.BlockSpec((TILE, PAIR), lambda i: (i, 0)),
            pl.BlockSpec((both, TILE), lambda i: (0, start + i)),
        ]
        + earlier_specs
        + [pl.BlockSpec(memory_space=pl.ANY)] * len(deps),
        out_specs=out_specs,
        scratch_shapes=scratch + [pltpu.VMEM((PAIR, both), BF16)],
        compiler_params=pltpu.CompilerParams(vmem_limit_bytes=48 * 2**20),
        cost_estimate=pl.CostEstimate(
            flops=24 * both * both * PAIR, bytes_accessed=16 * both * both, transcendentals=2 * both * both
        ),
    )(slopes[2 * pair : 2 * pair + 2], qkv, qkv, qkv, grad, logd, *earlier, *deps)


def on_device(tokens, qkv_weight, grad_attn, positions, slopes):
    rows, model = tokens.shape
    blocks = lax.axis_size("ctx")
    far_mask = blocks // 2
    bits = far_mask.bit_length() - 1
    me = lax.axis_index("ctx")
    side = me // far_mask
    head_side = lax.axis_index("head")
    shard, _, local_width = qkv_weight.shape
    width = local_width // 2
    heads = slopes.shape[0] // 2
    pairs = width // PAIR
    half_rows = rows // 2
    quarter = half_rows // 2

    def bit_of(position):
        return (me // 2**position) % 2

    def widen(stacked, position):
        arrived = flip(stacked, "ctx", 2**position)
        pieces = (stacked[:, :, None], arrived[:, :, None])
        along = [jnp.concatenate(c, 2) for c in (pieces, pieces[::-1])]
        stacked = jnp.where(bit_of(position) == 0, along[0], along[1])
        return stacked.reshape(2, -1, shard, 3 * width)

    with jax.named_scope("gather_weight"):
        weight_parts = []
        for which in (side, 1 - side):
            part = lax.dynamic_slice_in_dim(qkv_weight, which * width, width, 2)
            part = part.reshape(shard, 3, pairs, PAIR).transpose(0, 2, 1, 3)
            weight_parts.append(part.reshape(shard, 3 * width))
        far_positions = flip(positions, "ctx", far_mask)
        weight_far = flip(weight_parts[1], "ctx", far_mask)
        stacked = ordered(weight_parts[0][None], weight_far[None], side)[:, None]
        stacked, token_source = lax.optimization_barrier((stacked, tokens))
        for position in reversed(range(bits)):
            stacked = widen(stacked, position)
        weight = stacked.reshape(model, 3 * width)

    with jax.named_scope("exchange_inputs"):
        token_half = lax.dynamic_slice_in_dim(token_source, head_side * half_rows, half_rows, 0)
        near, cross = [], []
        for part in range(2):
            arrived = flip(token_half[part * quarter : (part + 1) * quarter], "ctx", far_mask)
            near.append(arrived)
            cross.append(flip(arrived, "head", 1))
        far_tokens = ordered(jnp.concatenate(near, 0), jnp.concatenate(cross, 0), head_side)
        grad_mine = lax.dynamic_slice_in_dim(grad_attn, side * width, width, 1)
        grad_theirs = lax.dynamic_slice_in_dim(grad_attn, (1 - side) * width, width, 1)
        first_theirs, _ = lax.optimization_barrier((grad_theirs[:, :PAIR], near[0]))
        grad_far = [flip(first_theirs, "ctx", far_mask)]
        slopes_mine = lax.dynamic_slice_in_dim(slopes, side * heads, heads, 0)

    with jax.named_scope("log_distance"):
        pos = jnp.concatenate([positions, far_positions], 0)
        logd = jnp.log(jnp.abs(pos[:, None] - pos[None, :]).astype(F32) + 1.0) * LOG2E

    with jax.named_scope("project"):
        qkv_own = jnp.dot(tokens, weight, preferred_element_type=F32).astype(BF16)
        qkv_far = jnp.dot(far_tokens, weight, preferred_element_type=F32).astype(BF16)
        qkv = jnp.concatenate([qkv_own, qkv_far], 0)
        both_tokens = jnp.concatenate([tokens, far_tokens], 0)

    late_mine, late_theirs, *late_grads = lax.optimization_barrier(
        (weight_parts[0], weight_parts[1], *[grad_theirs[:, p * PAIR : (p + 1) * PAIR] for p in range(1, pairs)], qkv_own)
    )[:-1]
    with jax.named_scope("exchange_inputs"):
        grad_far += [flip(g, "ctx", far_mask) for g in late_grads]
    with jax.named_scope("gather_other_weight"):
        back = flip(late_mine, "ctx", far_mask)
        stacked = ordered(late_theirs[None], back[None], side)[:, None]
    positions_left = list(reversed(range(bits)))

    def reduce_weight(total, position):
        bit = bit_of(position)
        folded = total.reshape(2, total.shape[1] // 2, 2, shard, total.shape[-1])
        send = lax.dynamic_index_in_dim(folded, 1 - bit, 2, keepdims=False)
        keep = lax.dynamic_index_in_dim(folded, bit, 2, keepdims=False)
        return keep + flip(send, "ctx", 2**position)

    deps = [stacked] + grad_far[1:]
    wholes, others, terms = [], [], []
    for pair in range(pairs):
        cut = slice(pair * PAIR, (pair + 1) * PAIR)
        with jax.named_scope("attention_far_queries"):
            far_dq, *sums = attention(
                True, pair, slopes_mine, qkv, grad_far[pair], logd, [], deps if pair else []
            )
        if pair:
            deps = [other_rest]
        with jax.named_scope("return_grads"):
            other_dq = flip(far_dq, "ctx", far_mask)
        if positions_left and pair:
            with jax.named_scope("gather_other_weight"):
                stacked = widen(stacked, positions_left.pop(0))
            with jax.named_scope("weight_grad"):
                terms[0] = reduce_weight(terms[0], 0)
            deps += [stacked, terms[0]]
        with jax.named_scope("attention_own_queries"):
            whole, far_rest = attention(
                False, pair, slopes_mine, qkv, grad_mine[:, cut], logd, [far_dq, *sums], deps
            )
        deps = [other_dq]
        if positions_left and not pair:
            with jax.named_scope("gather_other_weight"):
                stacked = widen(stacked, positions_left.pop(0))
                deps.append(stacked)
        with jax.named_scope("return_grads"):
            other_rest = flip(far_rest, "ctx", far_mask)
        wholes.append(whole)
        others.append(jnp.concatenate([other_dq, other_rest], 1))
        with jax.named_scope("weight_grad"):
            term = lax.dot_general(both_tokens, whole, (((0,), (0,)), ((), ())), preferred_element_type=F32)
            terms.append(term.reshape(2, far_mask, shard, 3 * PAIR))

    with jax.named_scope("gather_other_weight"):
        for position in positions_left:
            stacked = widen(stacked, position)
        weight_other = stacked.reshape(model, 3 * width)

    with jax.named_scope("weight_grad"):
        kept, arrived = [], []
        for pair, total in enumerate(terms):
            for position in range(0 if pair else 1, bits):
                total = reduce_weight(total, position)
            total = total.reshape(2, shard, 3 * PAIR)
            kept.append(lax.dynamic_index_in_dim(total, side, 0, keepdims=False))
            arrived.append(flip(lax.dynamic_index_in_dim(total, 1 - side, 0, keepdims=False), "ctx", far_mask))
        kept, arrived = [
            jnp.stack([t.reshape(shard, 3, PAIR) for t in side_terms], 2).reshape(shard, 3, width)
            for side_terms in (kept, arrived)
        ]
        d_weight = jnp.where(
            side == 0, jnp.concatenate([kept, arrived], 2), jnp.concatenate([arrived, kept], 2)
        )

    with jax.named_scope("token_grad"):
        dqkv = jnp.concatenate([w[:rows] for w in wholes] + others, 1)
        joined = jnp.concatenate([weight, weight_other], 1)

        def partial_rows(part):
            rows_part = lax.dynamic_slice_in_dim(dqkv, part * half_rows, half_rows, 0)
            return lax.dot_general(rows_part, joined, (((1,), (1,)), ((), ())), preferred_element_type=F32)

        sent = partial_rows(1 - head_side)
        kept = partial_rows(head_side)
        mine, cross = [], []
        for part in range(2):
            cut = slice(part * quarter, (part + 1) * quarter)
            total = (kept[cut] + flip(sent[cut], "head", 1)).astype(BF16)
            mine.append(total)
            cross.append(flip(total, "head", 1))
        d_tokens = ordered(jnp.concatenate(mine, 0), jnp.concatenate(cross, 0), head_side)
    return (d_tokens, d_weight)


def solution(mesh):
    placed = (P("ctx", None), P("ctx", None, "head"), P("ctx", "head"), P("ctx"), P("head"))
    return jax.shard_map(
        on_device,
        mesh=mesh,
        in_specs=placed,
        out_specs=(P("ctx", None), P("ctx", None, "head")),
        check_vma=False,
    )
```

```python
import functools
import math

import jax
import jax.numpy as jnp
from jax import lax
from jax.experimental import pallas as pl
from jax.experimental.pallas import tpu as pltpu
from jax.sharding import PartitionSpec as P

F32 = jnp.float32
BF16 = jnp.bfloat16
LOG2E = math.log2(math.e)
PAIR = 128
TILE = 256


def flip(value, axis, mask):
    pairs = [(source, source ^ mask) for source in range(lax.axis_size(axis))]
    return lax.ppermute(value, axis, pairs)


def after(value, *others):
    return lax.optimization_barrier((value, *others))[0]


def ordered(mine, other, bit):
    first = jnp.concatenate([mine, other], 0)
    second = jnp.concatenate([other, mine], 0)
    return jnp.where(bit == 0, first, second)


def attention_kernel(first, deps, *refs):
    slope_ref, q_ref, k_ref, v_ref, g_ref, logd_ref = refs[:6]
    rest = refs[6:]
    if first:
        dq_ref, dk_acc, dv_acc, kt_ref = rest[deps:]
    else:
        far_dq_ref, dk_in, dv_in = rest[:3]
        whole_ref, *far_refs, dk_acc, dv_acc, kt_ref = rest[3 + deps :]
    step = pl.program_id(0)
    steps = pl.num_programs(0)
    size = PAIR // 2
    scale = size ** (-0.5)

    @pl.when(step == 0)
    def _():
        kt_ref[...] = k_ref[...].astype(F32).T.astype(BF16)
        if first:
            dk_acc[...] = jnp.zeros_like(dk_acc)
            dv_acc[...] = jnp.zeros_like(dv_acc)
        else:
            dk_acc[...] = dk_in[...]
            dv_acc[...] = dv_in[...]

    lane = lax.broadcasted_iota(jnp.int32, (TILE, PAIR), 1)
    key = k_ref[...]
    key_t = kt_ref[...]
    value = v_ref[...]
    query = q_ref[...].astype(F32)
    grad = g_ref[...].astype(F32)
    contract_last = (((1,), (1,)), ((), ()))
    grads_q = []
    for head in range(2):
        here = (lane >= head * size) & (lane < (head + 1) * size)
        q_head = jnp.where(here, query, 0.0).astype(BF16)
        g_head = jnp.where(here, grad, 0.0)
        g_scaled = (g_head * scale).astype(BF16)
        g_head = g_head.astype(BF16)
        score = lax.dot_general(key, q_head, contract_last, preferred_element_type=F32)
        score = score * (scale * LOG2E) - logd_ref[...] * slope_ref[head]
        top = jnp.max(score, axis=0, keepdims=True)
        expd = jnp.exp2(score - top)
        inverse = 1.0 / jnp.sum(expd, axis=0, keepdims=True)
        prob = expd * inverse
        prob_round = prob.astype(BF16)
        dprob = lax.dot_general(value, g_scaled, contract_last, preferred_element_type=F32)
        delta = jnp.sum(prob_round.astype(F32) * dprob, axis=0, keepdims=True)
        dscore = (prob * (dprob - delta)).astype(BF16)
        dv_acc[...] += jnp.dot(prob_round, g_head, preferred_element_type=F32)
        dk_acc[...] += jnp.dot(dscore, q_head, preferred_element_type=F32)
        grad_q = jnp.dot(key_t, dscore, preferred_element_type=F32)
        grads_q.append(grad_q[head * size : (head + 1) * size])
    grad_q = jnp.concatenate(grads_q, 0).T.astype(BF16)

    if first:
        dq_ref[...] = grad_q
        return

    whole_ref[pl.ds(pl.multiple_of(step * TILE, TILE), TILE), :PAIR] = grad_q

    @pl.when(step == steps - 1)
    def _():
        rows = far_dq_ref.shape[0]
        dk = dk_acc[...].astype(BF16)
        dv = dv_acc[...].astype(BF16)
        whole_ref[rows:, :PAIR] = far_dq_ref[...]
        whole_ref[:, PAIR : 2 * PAIR] = dk
        whole_ref[:, 2 * PAIR :] = dv
        size = rows // len(far_refs)
        for number, far_ref in enumerate(far_refs):
            cut = slice(rows + number * size, rows + (number + 1) * size)
            far_ref[:, :PAIR] = dk[cut]
            far_ref[:, PAIR:] = dv[cut]


def attention(first, pair, slopes, qkv, grad, logd, earlier, deps, parts):
    both, _ = qkv.shape
    rows = both // 2
    steps = rows // TILE
    start = steps if first else 0
    acc = jax.ShapeDtypeStruct((both, PAIR), F32)
    fixed = lambda *shape: pl.BlockSpec(shape, lambda i: (0, 0))
    out_bf16 = lambda *shape: jax.ShapeDtypeStruct(shape, BF16)
    if first:
        out_shape = (out_bf16(rows, PAIR), acc, acc)
        out_specs = (pl.BlockSpec((TILE, PAIR), lambda i: (i, 0)), fixed(both, PAIR), fixed(both, PAIR))
        scratch = []
        earlier_specs = []
    else:
        out_shape = (out_bf16(both, 3 * PAIR),) + (out_bf16(rows // parts, 2 * PAIR),) * parts
        out_specs = (fixed(both, 3 * PAIR),) + (fixed(rows // parts, 2 * PAIR),) * parts
        scratch = [pltpu.VMEM((both, PAIR), F32), pltpu.VMEM((both, PAIR), F32)]
        earlier_specs = [fixed(rows, PAIR), fixed(both, PAIR), fixed(both, PAIR)]
    return pl.pallas_call(
        functools.partial(attention_kernel, first, len(deps)),
        grid=(steps,),
        out_shape=out_shape,
        in_specs=[
            pl.BlockSpec(memory_space=pltpu.SMEM),
            pl.BlockSpec((TILE, PAIR), lambda i: (start + i, 3 * pair)),
            pl.BlockSpec((both, PAIR), lambda i: (0, 3 * pair + 1)),
            pl.BlockSpec((both, PAIR), lambda i: (0, 3 * pair + 2)),
            pl.BlockSpec((TILE, PAIR), lambda i: (i, 0)),
            pl.BlockSpec((both, TILE), lambda i: (0, start + i)),
        ]
        + earlier_specs
        + [pl.BlockSpec(memory_space=pl.ANY)] * len(deps),
        out_specs=out_specs,
        scratch_shapes=scratch + [pltpu.VMEM((PAIR, both), BF16)],
        compiler_params=pltpu.CompilerParams(vmem_limit_bytes=48 * 2**20),
        cost_estimate=pl.CostEstimate(
            flops=24 * both * both * PAIR, bytes_accessed=16 * both * both, transcendentals=2 * both * both
        ),
    )(slopes[2 * pair : 2 * pair + 2], qkv, qkv, qkv, grad, logd, *earlier, *deps)


def on_device(tokens, qkv_weight, grad_attn, positions, slopes):
    rows, model = tokens.shape
    blocks = lax.axis_size("ctx")
    far_mask = blocks // 2
    bits = far_mask.bit_length() - 1
    me = lax.axis_index("ctx")
    side = me // far_mask
    head_side = lax.axis_index("head")
    shard, _, local_width = qkv_weight.shape
    width = local_width // 2
    heads = slopes.shape[0] // 2
    pairs = width // PAIR
    half_rows = rows // 2

    def bit_of(position):
        return (me // 2**position) % 2

    def widen(stacked, position):
        arrived = flip(stacked, "ctx", 2**position)
        pieces = (stacked[:, :, None], arrived[:, :, None])
        along = [jnp.concatenate(c, 2) for c in (pieces, pieces[::-1])]
        stacked = jnp.where(bit_of(position) == 0, along[0], along[1])
        return stacked.reshape(2, -1, shard, 6 * width)

    def by_side(columns):
        return [lax.dynamic_slice_in_dim(columns, which * 3 * width, 3 * width, 1) for which in (side, 1 - side)]

    with jax.named_scope("exchange_inputs"):
        grad_mine = lax.dynamic_slice_in_dim(grad_attn, side * width, width, 1)
        grad_theirs = lax.dynamic_slice_in_dim(grad_attn, (1 - side) * width, width, 1)
        far_positions = flip(positions, "ctx", far_mask)
        slopes_mine = lax.dynamic_slice_in_dim(slopes, side * heads, heads, 0)

    with jax.named_scope("gather_weight"):
        part = qkv_weight.reshape(shard, 3, 2, pairs, PAIR).transpose(0, 2, 3, 1, 4).reshape(shard, 6 * width)
        stacked = ordered(part[None], flip(part, "ctx", far_mask)[None], side)[:, None]
        stacked, token_source = lax.optimization_barrier((stacked, tokens))
        for position in reversed(range(bits)):
            stacked = widen(stacked, position)
        weight_all = stacked.reshape(model, 6 * width)
        weight, weight_other = by_side(weight_all)

    with jax.named_scope("exchange_inputs"):
        grad_far = [flip(grad_theirs[:, :PAIR], "ctx", far_mask)]
        token_half = lax.dynamic_slice_in_dim(token_source, head_side * half_rows, half_rows, 0)
        piece = half_rows // 3
        near, cross = [], []
        for number in range(3):
            arrived = flip(token_half[number * piece : (number + 1) * piece], "ctx", far_mask)
            near.append(arrived)
            cross.append(flip(arrived, "head", 1))
        far_tokens = ordered(jnp.concatenate(near, 0), jnp.concatenate(cross, 0), head_side)

    with jax.named_scope("log_distance"):
        pos = jnp.concatenate([positions, far_positions], 0)
        logd = jnp.log(jnp.abs(pos[:, None] - pos[None, :]).astype(F32) + 1.0) * LOG2E

    with jax.named_scope("project"):
        qkv_own = jnp.dot(tokens, weight, preferred_element_type=F32).astype(BF16)
        qkv_far = jnp.dot(far_tokens, weight, preferred_element_type=F32).astype(BF16)
        qkv = jnp.concatenate([qkv_own, qkv_far], 0)
        both_tokens = jnp.concatenate([tokens, far_tokens], 0)

    with jax.named_scope("exchange_inputs"):
        late_grad, _ = lax.optimization_barrier((grad_theirs[:, PAIR:], qkv_own))
        grad_far += [flip(late_grad[:, p * PAIR : (p + 1) * PAIR], "ctx", far_mask) for p in range(pairs - 1)]

    with jax.named_scope("gather_other_weight"):
        core = bit_of(0)
        core_half = lax.dynamic_slice_in_dim(weight_all, core * (model // 2), model // 2, 0)
        core_half = after(core_half, qkv_own)
        across_first = flip(core_half[: model // 4], "head", 1)

    def reduce_weight(total, position):
        bit = bit_of(position)
        folded = total.reshape(2, total.shape[1] // 2, 2, shard, total.shape[-1])
        send = lax.dynamic_index_in_dim(folded, 1 - bit, 2, keepdims=False)
        keep = lax.dynamic_index_in_dim(folded, bit, 2, keepdims=False)
        return keep + flip(send, "ctx", 2**position)

    def attend(first, pair, grad, earlier, deps, parts=1):
        with jax.named_scope("attention_far_queries" if first else "attention_own_queries"):
            return attention(first, pair, slopes_mine, qkv, grad, logd, earlier, deps, parts)

    def weight_term(whole):
        with jax.named_scope("weight_grad"):
            term = lax.dot_general(both_tokens, whole, (((0,), (0,)), ((), ())), preferred_element_type=F32)
            return term.reshape(2, far_mask, shard, 3 * PAIR)

    wholes, others, across_own, across_other, terms = [], [], [], [], []
    before_far, before_own = [], grad_far[1:] + [across_first]
    for pair in range(pairs):
        last = pair == pairs - 1
        cut = slice(pair * PAIR, (pair + 1) * PAIR)
        far_dq, *sums = attend(True, pair, grad_far[pair], [], before_far)
        with jax.named_scope("return_grads"):
            other_dq = flip(far_dq, "ctx", far_mask)
        if not pair:
            with jax.named_scope("gather_other_weight"):
                across_second = flip(after(core_half[model // 4 :], far_dq), "head", 1)
        if pair:
            with jax.named_scope("return_grads"):
                across_other[-1] = flip(after(others[-1], far_dq), "head", 1)
            with jax.named_scope("weight_grad"):
                terms[-1] = after(reduce_weight(terms[-1], 0), far_dq)
            before_own = [others[-1], across_own[-1], terms[-1]]
        parts = 2 if last else 1
        whole, *far_rest = attend(False, pair, grad_mine[:, cut], [far_dq, *sums], before_own, parts)
        before_far = [other_dq, across_second]
        with jax.named_scope("return_grads"):
            if pair:
                across_other[-1] = after(across_other[-1], whole)
                terms[-1] = after(reduce_weight(terms[-1], 1), whole)
            size = rows // parts
            rest = [flip(f, "ctx", far_mask) for f in far_rest]
            other = [jnp.concatenate([other_dq[n * size : (n + 1) * size], rest[n]], 1) for n in range(parts)]
            others.append(other[0] if parts == 1 else jnp.concatenate(other, 0))
            across = jnp.concatenate([flip(o, "head", 1) for o in other], 0) if last else None
            across_own.append(flip(whole[:rows], "head", 1))
        wholes.append(whole)
        across_other.append(across)
        terms.append(weight_term(whole))

    with jax.named_scope("gather_other_weight"):
        across_half = jnp.concatenate([across_first, across_second], 0)
        across_rest = flip(after(across_half, wholes[-1]), "ctx", 1)

    with jax.named_scope("weight_grad"):
        kept, arrived = [], []
        for pair, total in enumerate(terms):
            for position in range(0 if pair == pairs - 1 else 2, bits):
                total = reduce_weight(total, position)
            total = total.reshape(2, shard, 3 * PAIR)
            kept.append(lax.dynamic_index_in_dim(total, side, 0, keepdims=False))
            arrived.append(flip(lax.dynamic_index_in_dim(total, 1 - side, 0, keepdims=False), "ctx", far_mask))
        kept, arrived = [
            jnp.stack([t.reshape(shard, 3, PAIR) for t in side_terms], 2).reshape(shard, 3, width)
            for side_terms in (kept, arrived)
        ]
        d_weight = jnp.where(
            side == 0, jnp.concatenate([kept, arrived], 2), jnp.concatenate([arrived, kept], 2)
        )

    with jax.named_scope("token_grad"):
        across_all = ordered(across_half, across_rest, core)
        across_weight, across_weight_other = by_side(across_all)

        def product(pieces):
            left = jnp.concatenate([p for p, _ in pieces], 1)
            right = jnp.concatenate([w for _, w in pieces], 1)
            return lax.dot_general(left, right, (((1,), (1,)), ((), ())), preferred_element_type=F32)

        total = None
        for pair in range(pairs):
            cut = slice(pair * 3 * PAIR, (pair + 1) * 3 * PAIR)
            early = [(wholes[pair][:rows], weight[:, cut]), (across_own[pair], across_weight[:, cut])]
            late = [(others[pair], weight_other[:, cut]), (across_other[pair], across_weight_other[:, cut])]
            for pieces in ([early, late] if pair == pairs - 1 else [early + late]):
                term = product(pieces)
                total = term if total is None else total + term
        d_tokens = total.astype(BF16)
    return (d_tokens, d_weight)


def solution(mesh):
    placed = (P("ctx", None), P("ctx", None, "head"), P("ctx", "head"), P("ctx"), P("head"))
    return jax.shard_map(
        on_device,
        mesh=mesh,
        in_specs=placed,
        out_specs=(P("ctx", None), P("ctx", None, "head")),
        check_vma=False,
    )
```

```python
import functools
import math

import jax
import jax.numpy as jnp
from jax import lax
from jax.experimental import pallas as pl
from jax.experimental.pallas import tpu as pltpu
from jax.sharding import PartitionSpec as P

F32 = jnp.float32
BF16 = jnp.bfloat16
LOG2E = math.log2(math.e)
PAIR = 128
TILE = 256


def flip(value, axis, mask):
    pairs = [(source, source ^ mask) for source in range(lax.axis_size(axis))]
    return lax.ppermute(value, axis, pairs)


def after(value, *others):
    return lax.optimization_barrier((value, *others))[0]


def ordered(mine, other, bit):
    first = jnp.concatenate([mine, other], 0)
    second = jnp.concatenate([other, mine], 0)
    return jnp.where(bit == 0, first, second)


def attention_kernel(last, start, held, done, deps, *refs):
    slope_ref, q_ref, k_ref, v_ref, g_ref, logd_ref = refs[:6]
    rest = refs[6:]
    sums_in, rest = rest[:held], rest[held:]
    dq_in, rest = rest[:done], rest[done + deps :]
    if last:
        whole_ref, *far_refs, dk_acc, dv_acc, kt_ref = rest
    else:
        dq_ref, dk_acc, dv_acc, kt_ref = rest
    step = pl.program_id(0)
    steps = pl.num_programs(0)
    size = PAIR // 2
    scale = size ** (-0.5)

    @pl.when(step == 0)
    def _():
        kt_ref[...] = k_ref[...].astype(F32).T.astype(BF16)
        if held:
            dk_acc[...] = sums_in[0][...]
            dv_acc[...] = sums_in[1][...]
        else:
            dk_acc[...] = jnp.zeros_like(dk_acc)
            dv_acc[...] = jnp.zeros_like(dv_acc)

    lane = lax.broadcasted_iota(jnp.int32, (TILE, PAIR), 1)
    key = k_ref[...]
    key_t = kt_ref[...]
    value = v_ref[...]
    query = q_ref[...].astype(F32)
    grad = g_ref[...].astype(F32)
    contract_last = (((1,), (1,)), ((), ()))
    grads_q = []
    for head in range(2):
        here = (lane >= head * size) & (lane < (head + 1) * size)
        q_head = jnp.where(here, query, 0.0).astype(BF16)
        g_head = jnp.where(here, grad, 0.0)
        g_scaled = (g_head * scale).astype(BF16)
        g_head = g_head.astype(BF16)
        score = lax.dot_general(key, q_head, contract_last, preferred_element_type=F32)
        score = score * (scale * LOG2E) - logd_ref[...] * slope_ref[head]
        top = jnp.max(score, axis=0, keepdims=True)
        expd = jnp.exp2(score - top)
        inverse = 1.0 / jnp.sum(expd, axis=0, keepdims=True)
        prob = expd * inverse
        prob_round = prob.astype(BF16)
        dprob = lax.dot_general(value, g_scaled, contract_last, preferred_element_type=F32)
        delta = jnp.sum(prob_round.astype(F32) * dprob, axis=0, keepdims=True)
        dscore = (prob * (dprob - delta)).astype(BF16)
        dv_acc[...] += jnp.dot(prob_round, g_head, preferred_element_type=F32)
        dk_acc[...] += jnp.dot(dscore, q_head, preferred_element_type=F32)
        grad_q = jnp.dot(key_t, dscore, preferred_element_type=F32)
        grads_q.append(grad_q[head * size : (head + 1) * size])
    grad_q = jnp.concatenate(grads_q, 0).T.astype(BF16)

    if not last:
        dq_ref[...] = grad_q
        return

    whole_ref[pl.ds(pl.multiple_of((start + step) * TILE, TILE), TILE), :PAIR] = grad_q

    @pl.when(step == steps - 1)
    def _():
        rows = whole_ref.shape[0] // 2
        dk = dk_acc[...].astype(BF16)
        dv = dv_acc[...].astype(BF16)
        whole_ref[rows:, :PAIR] = dq_in[0][...]
        if done > 1:
            whole_ref[: start * TILE, :PAIR] = dq_in[1][...]
        whole_ref[:, PAIR : 2 * PAIR] = dk
        whole_ref[:, 2 * PAIR :] = dv
        size = rows // len(far_refs)
        for number, far_ref in enumerate(far_refs):
            cut = slice(rows + number * size, rows + (number + 1) * size)
            far_ref[:, :PAIR] = dk[cut]
            far_ref[:, PAIR:] = dv[cut]


def attention(pair, start, stop, slopes, qkv, grad, logd, sums, dqs, deps, parts):
    both, _ = qkv.shape
    rows = both // 2
    steps = stop - start
    acc = jax.ShapeDtypeStruct((both, PAIR), F32)
    fixed = lambda *shape: pl.BlockSpec(shape, lambda i: (0, 0))
    out_bf16 = lambda *shape: jax.ShapeDtypeStruct(shape, BF16)
    if parts:
        out_shape = (out_bf16(both, 3 * PAIR),) + (out_bf16(rows // parts, 2 * PAIR),) * parts
        out_specs = (fixed(both, 3 * PAIR),) + (fixed(rows // parts, 2 * PAIR),) * parts
        scratch = [pltpu.VMEM((both, PAIR), F32), pltpu.VMEM((both, PAIR), F32)]
    else:
        out_shape = (out_bf16(steps * TILE, PAIR), acc, acc)
        out_specs = (pl.BlockSpec((TILE, PAIR), lambda i: (i, 0)), fixed(both, PAIR), fixed(both, PAIR))
        scratch = []
    return pl.pallas_call(
        functools.partial(attention_kernel, bool(parts), start, len(sums), len(dqs), len(deps)),
        grid=(steps,),
        out_shape=out_shape,
        in_specs=[
            pl.BlockSpec(memory_space=pltpu.SMEM),
            pl.BlockSpec((TILE, PAIR), lambda i: (start + i, 3 * pair)),
            pl.BlockSpec((both, PAIR), lambda i: (0, 3 * pair + 1)),
            pl.BlockSpec((both, PAIR), lambda i: (0, 3 * pair + 2)),
            pl.BlockSpec((TILE, PAIR), lambda i: (i, 0)),
            pl.BlockSpec((both, TILE), lambda i: (0, start + i)),
        ]
        + [fixed(both, PAIR)] * len(sums)
        + [fixed(*dq.shape) for dq in dqs]
        + [pl.BlockSpec(memory_space=pl.ANY)] * len(deps),
        out_specs=out_specs,
        scratch_shapes=scratch + [pltpu.VMEM((PAIR, both), BF16)],
        compiler_params=pltpu.CompilerParams(vmem_limit_bytes=48 * 2**20),
        cost_estimate=pl.CostEstimate(
            flops=24 * both * both * PAIR, bytes_accessed=16 * both * both, transcendentals=2 * both * both
        ),
    )(slopes[2 * pair : 2 * pair + 2], qkv, qkv, qkv, grad, logd, *sums, *dqs, *deps)


def assemble_kernel(side_ref, kept_ref, arrived_ref, _, out_ref):
    pairs = kept_ref.shape[1] // (3 * PAIR)
    for which in range(2):
        here = side_ref[0] == which
        for pair in range(pairs):
            for third in range(3):
                source = pl.ds((pair * 3 + third) * PAIR, PAIR)
                value = jnp.where(here, kept_ref[:, source], arrived_ref[:, source])
                out_ref[:, third, pl.ds((which * pairs + pair) * PAIR, PAIR)] = value


def assemble(side, kept, arrived, earlier):
    shard, columns = kept.shape
    vmem = pl.BlockSpec(memory_space=pltpu.VMEM)
    return pl.pallas_call(
        assemble_kernel,
        out_shape=jax.ShapeDtypeStruct((shard, 3, 2 * columns // 3), F32),
        in_specs=[pl.BlockSpec(memory_space=pltpu.SMEM), vmem, vmem, pl.BlockSpec(memory_space=pl.ANY)],
        out_specs=vmem,
    )(side.astype(jnp.int32).reshape(1), kept, arrived, earlier)


def on_device(tokens, qkv_weight, grad_attn, positions, slopes):
    rows, model = tokens.shape
    blocks = lax.axis_size("ctx")
    far_mask = blocks // 2
    bits = far_mask.bit_length() - 1
    me = lax.axis_index("ctx")
    side = me // far_mask
    head_side = lax.axis_index("head")
    shard, _, local_width = qkv_weight.shape
    width = local_width // 2
    heads = slopes.shape[0] // 2
    pairs = width // PAIR
    half_rows = rows // 2

    def bit_of(position):
        return (me // 2**position) % 2

    def widen(stacked, position):
        arrived = flip(stacked, "ctx", 2**position)
        pieces = (stacked[:, :, None], arrived[:, :, None])
        along = [jnp.concatenate(c, 2) for c in (pieces, pieces[::-1])]
        stacked = jnp.where(bit_of(position) == 0, along[0], along[1])
        return stacked.reshape(2, -1, shard, 6 * width)

    def by_side(columns):
        return [lax.dynamic_slice_in_dim(columns, which * 3 * width, 3 * width, 1) for which in (side, 1 - side)]

    with jax.named_scope("exchange_inputs"):
        grad_mine = lax.dynamic_slice_in_dim(grad_attn, side * width, width, 1)
        grad_theirs = lax.dynamic_slice_in_dim(grad_attn, (1 - side) * width, width, 1)
        far_positions = flip(positions, "ctx", far_mask)
        slopes_mine = lax.dynamic_slice_in_dim(slopes, side * heads, heads, 0)

    with jax.named_scope("gather_weight"):
        part = qkv_weight.reshape(shard, 3, 2, pairs, PAIR).transpose(0, 2, 3, 1, 4).reshape(shard, 6 * width)
        stacked = ordered(part[None], flip(part, "ctx", far_mask)[None], side)[:, None]
        for position in reversed(range(bits)):
            stacked = widen(stacked, position)
        weight_all = stacked.reshape(model, 6 * width)
        weight, weight_other = by_side(weight_all)

    with jax.named_scope("exchange_inputs"):
        token_half = lax.dynamic_slice_in_dim(tokens, head_side * half_rows, half_rows, 0)
        piece = half_rows // 3
        near, cross = [], []
        for number in range(3):
            source = token_half[number * piece : (number + 1) * piece]
            if number:
                source = after(source, near[-1])
            arrived = flip(source, "ctx", far_mask)
            near.append(arrived)
            cross.append(flip(arrived, "head", 1))
        grad_far = [flip(after(grad_theirs[:, :PAIR], near[1]), "ctx", far_mask)]
        far_tokens = ordered(jnp.concatenate(near, 0), jnp.concatenate(cross, 0), head_side)

    with jax.named_scope("log_distance"):
        pos = jnp.concatenate([positions, far_positions], 0)
        logd = jnp.log(jnp.abs(pos[:, None] - pos[None, :]).astype(F32) + 1.0) * LOG2E

    with jax.named_scope("project"):
        qkv_own = jnp.dot(tokens, weight, preferred_element_type=F32).astype(BF16)
        qkv_far = jnp.dot(far_tokens, weight, preferred_element_type=F32).astype(BF16)
        qkv = jnp.concatenate([qkv_own, qkv_far], 0)
        both_tokens = jnp.concatenate([tokens, far_tokens], 0)

    with jax.named_scope("exchange_inputs"):
        late_grad, _ = lax.optimization_barrier((grad_theirs[:, PAIR:], qkv_own))
        grad_far += [flip(late_grad[:, p * PAIR : (p + 1) * PAIR], "ctx", far_mask) for p in range(pairs - 1)]

    with jax.named_scope("gather_other_weight"):
        core = bit_of(0)
        core_half = lax.dynamic_slice_in_dim(weight_all, core * (model // 2), model // 2, 0)
        core_half = after(core_half, qkv_own)
        across_first = flip(core_half[: model // 4], "head", 1)

    tiles = rows // TILE

    def attend(pair, start, stop, grad, sums, dqs, deps, parts=0):
        with jax.named_scope("attention"):
            return attention(pair, start, stop, slopes_mine, qkv, grad, logd, sums, dqs, deps, parts)

    wholes, others, across_own, across_other = [], [], [], []
    before_far, before_own = [], grad_far[1:] + [across_first]
    for pair in range(pairs):
        last = pair == pairs - 1
        cut = slice(pair * PAIR, (pair + 1) * PAIR)
        far_dq, *sums = attend(pair, tiles, 2 * tiles, grad_far[pair], [], [], before_far)
        with jax.named_scope("return_grads"):
            other_dq = flip(far_dq, "ctx", far_mask)
        if not pair:
            with jax.named_scope("gather_other_weight"):
                across_second = flip(after(core_half[model // 4 :], far_dq), "head", 1)
        if pair:
            with jax.named_scope("return_grads"):
                across_other[-1] = flip(after(others[-1], far_dq), "head", 1)
            before_own = [others[-1], across_own[-1], across_second]
        parts = 2 if last else 1
        dqs, begin = [far_dq], 0
        if last:
            begin = tiles - 1
            own_dq, *sums = attend(pair, 0, begin, grad_mine[: begin * TILE, cut], sums, [], before_own)
            dqs.append(own_dq)
            before_own = [across_other[-1], other_dq]
        whole, *far_rest = attend(pair, begin, tiles, grad_mine[begin * TILE :, cut], sums, dqs, before_own, parts)
        before_far = [other_dq]
        with jax.named_scope("return_grads"):
            size = rows // parts
            rest = [flip(f, "ctx", far_mask) for f in far_rest]
            others.append(None if last else jnp.concatenate([other_dq, rest[0]], 1))
            across_own.append(flip(whole[:rows], "head", 1))
        wholes.append(whole)
        across_other.append(None)

    with jax.named_scope("gather_other_weight"):
        across_half = jnp.concatenate([across_first, across_second], 0)
        across_rest = flip(after(across_half, wholes[-1]), "ctx", 1)

    with jax.named_scope("weight_grad"):
        total = lax.dot_general(
            both_tokens, jnp.concatenate(wholes, 1), (((0,), (0,)), ((), ())), preferred_element_type=F32
        ).reshape(2, far_mask // 2, 2, shard, 3 * width)
        total = lax.dynamic_index_in_dim(total, core, 2, keepdims=False) + flip(
            lax.dynamic_index_in_dim(total, 1 - core, 2, keepdims=False), "ctx", 1
        )
        group = (me % far_mask) // 2
        pieces = [lax.dynamic_index_in_dim(total, group, 1, keepdims=False)]
        sends = [
            lax.dynamic_index_in_dim(total, jnp.bitwise_xor(group, apart), 1, keepdims=False)
            for apart in range(1, far_mask // 2)
        ]
        pieces += [flip(send, "ctx", 2 * (n + 1)) for n, send in enumerate(sends)]
        total = sum(pieces[1:], pieces[0])

    with jax.named_scope("return_grads"):
        rest = [after(arrived, *sends) for arrived in rest]
        other = [jnp.concatenate([other_dq[n * size : (n + 1) * size], r], 1) for n, r in enumerate(rest)]
        others[-1] = jnp.concatenate(other, 0)
        across_other[-1] = jnp.concatenate([flip(o, "head", 1) for o in other], 0)

    with jax.named_scope("token_grad"):
        across_all = ordered(across_half, across_rest, core)
        across_weight, across_weight_other = by_side(across_all)

        def product(pieces):
            left = jnp.concatenate([p for p, _ in pieces], 1)
            right = jnp.concatenate([w for _, w in pieces], 1)
            return lax.dot_general(left, right, (((1,), (1,)), ((), ())), preferred_element_type=F32)

        rows_sum = None
        for pair in range(pairs):
            cut = slice(pair * 3 * PAIR, (pair + 1) * 3 * PAIR)
            early = [(wholes[pair][:rows], weight[:, cut]), (across_own[pair], across_weight[:, cut])]
            late = [(others[pair], weight_other[:, cut]), (across_other[pair], across_weight_other[:, cut])]
            if pair < pairs - 1:
                early = early + late
            term = product(early)
            rows_sum = term if rows_sum is None else rows_sum + term
        d_tokens = (rows_sum + product(late)).astype(BF16)

    with jax.named_scope("weight_grad"):
        total = after(total, rows_sum)
        kept = lax.dynamic_index_in_dim(total, side, 0, keepdims=False)
        arrived = flip(lax.dynamic_index_in_dim(total, 1 - side, 0, keepdims=False), "ctx", far_mask)
        d_weight = assemble(side, kept, arrived, d_tokens)
    return (d_tokens, d_weight)


def solution(mesh):
    placed = (P("ctx", None), P("ctx", None, "head"), P("ctx", "head"), P("ctx"), P("head"))
    return jax.shard_map(
        on_device,
        mesh=mesh,
        in_specs=placed,
        out_specs=(P("ctx", None), P("ctx", None, "head")),
        check_vma=False,
    )
```

```python
import functools
import math

import jax
import jax.numpy as jnp
from jax import lax
from jax.experimental import pallas as pl
from jax.experimental.pallas import tpu as pltpu
from jax.sharding import PartitionSpec as P

F32 = jnp.float32
BF16 = jnp.bfloat16
LOG2E = math.log2(math.e)
PAIR = 128
TILE = 256


def flip(value, axis, mask):
    pairs = [(source, source ^ mask) for source in range(lax.axis_size(axis))]
    return lax.ppermute(value, axis, pairs)


def after(value, *others):
    return lax.optimization_barrier((value, *others))[0]


def ordered(mine, other, bit):
    first = jnp.concatenate([mine, other], 0)
    second = jnp.concatenate([other, mine], 0)
    return jnp.where(bit == 0, first, second)


def attention_kernel(last, start, held, done, deps, *refs):
    slope_ref, q_ref, k_ref, v_ref, g_ref, logd_ref = refs[:6]
    rest = refs[6:]
    sums_in, rest = rest[:held], rest[held:]
    dq_in, rest = rest[:done], rest[done + deps :]
    if last:
        whole_ref, *far_refs, dk_acc, dv_acc, kt_ref = rest
    else:
        dq_ref, dk_acc, dv_acc, kt_ref = rest
    step = pl.program_id(0)
    steps = pl.num_programs(0)
    size = PAIR // 2
    scale = size ** (-0.5)

    @pl.when(step == 0)
    def _():
        kt_ref[...] = k_ref[...].astype(F32).T.astype(BF16)
        if held:
            dk_acc[...] = sums_in[0][...]
            dv_acc[...] = sums_in[1][...]
        else:
            dk_acc[...] = jnp.zeros_like(dk_acc)
            dv_acc[...] = jnp.zeros_like(dv_acc)

    lane = lax.broadcasted_iota(jnp.int32, (TILE, PAIR), 1)
    key = k_ref[...]
    key_t = kt_ref[...]
    value = v_ref[...]
    query = q_ref[...].astype(F32)
    grad = g_ref[...].astype(F32)
    contract_last = (((1,), (1,)), ((), ()))
    queries, grads, scores, dprobs = [], [], [], []
    for head in range(2):
        here = (lane >= head * size) & (lane < (head + 1) * size)
        queries.append(jnp.where(here, query, 0.0).astype(BF16))
        g_head = jnp.where(here, grad, 0.0)
        grads.append(g_head.astype(BF16))
        scores.append(lax.dot_general(key, queries[head], contract_last, preferred_element_type=F32))
        g_scaled = (g_head * scale).astype(BF16)
        dprobs.append(lax.dot_general(value, g_scaled, contract_last, preferred_element_type=F32))
    probs, dscores, grads_q = [], [], []
    for head in range(2):
        score = scores[head] * (scale * LOG2E) - logd_ref[...] * slope_ref[head]
        top = jnp.max(score, axis=0, keepdims=True)
        expd = jnp.exp2(score - top)
        inverse = 1.0 / jnp.sum(expd, axis=0, keepdims=True)
        prob = expd * inverse
        prob_round = prob.astype(BF16)
        dprob = dprobs[head]
        delta = jnp.sum(prob_round.astype(F32) * dprob, axis=0, keepdims=True)
        dscore = (prob * (dprob - delta)).astype(BF16)
        probs.append(prob_round)
        dscores.append(dscore)
        grad_q = jnp.dot(key_t, dscore, preferred_element_type=F32)
        grads_q.append(grad_q[head * size : (head + 1) * size])
    dv_acc[...] += jnp.dot(jnp.concatenate(probs, 1), jnp.concatenate(grads, 0), preferred_element_type=F32)
    dk_acc[...] += jnp.dot(jnp.concatenate(dscores, 1), jnp.concatenate(queries, 0), preferred_element_type=F32)
    grad_q = jnp.concatenate(grads_q, 0).T.astype(BF16)

    if not last:
        dq_ref[...] = grad_q
        return

    whole_ref[pl.ds(pl.multiple_of((start + step) * TILE, TILE), TILE), :PAIR] = grad_q

    @pl.when(step == steps - 1)
    def _():
        rows = whole_ref.shape[0] // 2
        dk = dk_acc[...].astype(BF16)
        dv = dv_acc[...].astype(BF16)
        whole_ref[rows:, :PAIR] = dq_in[0][...]
        if done > 1:
            whole_ref[: start * TILE, :PAIR] = dq_in[1][...]
        whole_ref[:, PAIR : 2 * PAIR] = dk
        whole_ref[:, 2 * PAIR :] = dv
        size = rows // len(far_refs)
        for number, far_ref in enumerate(far_refs):
            cut = slice(rows + number * size, rows + (number + 1) * size)
            far_ref[:, :PAIR] = dk[cut]
            far_ref[:, PAIR:] = dv[cut]


def attention(pair, start, stop, slopes, qkv, grad, logd, sums, dqs, deps, parts):
    both, _ = qkv.shape
    rows = both // 2
    steps = stop - start
    acc = jax.ShapeDtypeStruct((both, PAIR), F32)
    fixed = lambda *shape: pl.BlockSpec(shape, lambda i: (0, 0))
    out_bf16 = lambda *shape: jax.ShapeDtypeStruct(shape, BF16)
    if parts:
        out_shape = (out_bf16(both, 3 * PAIR),) + (out_bf16(rows // parts, 2 * PAIR),) * parts
        out_specs = (fixed(both, 3 * PAIR),) + (fixed(rows // parts, 2 * PAIR),) * parts
        scratch = [pltpu.VMEM((both, PAIR), F32), pltpu.VMEM((both, PAIR), F32)]
    else:
        out_shape = (out_bf16(steps * TILE, PAIR), acc, acc)
        out_specs = (pl.BlockSpec((TILE, PAIR), lambda i: (i, 0)), fixed(both, PAIR), fixed(both, PAIR))
        scratch = []
    return pl.pallas_call(
        functools.partial(attention_kernel, bool(parts), start, len(sums), len(dqs), len(deps)),
        grid=(steps,),
        out_shape=out_shape,
        in_specs=[
            pl.BlockSpec(memory_space=pltpu.SMEM),
            pl.BlockSpec((TILE, PAIR), lambda i: (start + i, 3 * pair)),
            pl.BlockSpec((both, PAIR), lambda i: (0, 3 * pair + 1)),
            pl.BlockSpec((both, PAIR), lambda i: (0, 3 * pair + 2)),
            pl.BlockSpec((TILE, PAIR), lambda i: (i, 0)),
            pl.BlockSpec((both, TILE), lambda i: (0, start + i)),
        ]
        + [fixed(both, PAIR)] * len(sums)
        + [fixed(*dq.shape) for dq in dqs]
        + [pl.BlockSpec(memory_space=pl.ANY)] * len(deps),
        out_specs=out_specs,
        scratch_shapes=scratch + [pltpu.VMEM((PAIR, both), BF16)],
        compiler_params=pltpu.CompilerParams(vmem_limit_bytes=48 * 2**20),
        cost_estimate=pl.CostEstimate(
            flops=24 * both * both * PAIR, bytes_accessed=16 * both * both, transcendentals=2 * both * both
        ),
    )(slopes[2 * pair : 2 * pair + 2], qkv, qkv, qkv, grad, logd, *sums, *dqs, *deps)


def assemble_kernel(side_ref, kept_ref, arrived_ref, _, out_ref):
    pairs = kept_ref.shape[1] // (3 * PAIR)
    for which in range(2):
        here = side_ref[0] == which
        for pair in range(pairs):
            for third in range(3):
                source = pl.ds((pair * 3 + third) * PAIR, PAIR)
                value = jnp.where(here, kept_ref[:, source], arrived_ref[:, source])
                out_ref[:, third, pl.ds((which * pairs + pair) * PAIR, PAIR)] = value


def assemble(side, kept, arrived, earlier):
    shard, columns = kept.shape
    vmem = pl.BlockSpec(memory_space=pltpu.VMEM)
    return pl.pallas_call(
        assemble_kernel,
        out_shape=jax.ShapeDtypeStruct((shard, 3, 2 * columns // 3), F32),
        in_specs=[pl.BlockSpec(memory_space=pltpu.SMEM), vmem, vmem, pl.BlockSpec(memory_space=pl.ANY)],
        out_specs=vmem,
    )(side.astype(jnp.int32).reshape(1), kept, arrived, earlier)


def on_device(tokens, qkv_weight, grad_attn, positions, slopes):
    rows, model = tokens.shape
    blocks = lax.axis_size("ctx")
    far_mask = blocks // 2
    bits = far_mask.bit_length() - 1
    me = lax.axis_index("ctx")
    side = me // far_mask
    head_side = lax.axis_index("head")
    shard, _, local_width = qkv_weight.shape
    width = local_width // 2
    heads = slopes.shape[0] // 2
    pairs = width // PAIR
    half_rows = rows // 2

    def bit_of(position):
        return (me // 2**position) % 2

    def widen(stacked, position):
        arrived = flip(stacked, "ctx", 2**position)
        pieces = (stacked[:, :, None], arrived[:, :, None])
        along = [jnp.concatenate(c, 2) for c in (pieces, pieces[::-1])]
        stacked = jnp.where(bit_of(position) == 0, along[0], along[1])
        return stacked.reshape(2, -1, shard, 6 * width)

    def by_side(columns):
        return [lax.dynamic_slice_in_dim(columns, which * 3 * width, 3 * width, 1) for which in (side, 1 - side)]

    with jax.named_scope("exchange_inputs"):
        grad_mine = lax.dynamic_slice_in_dim(grad_attn, side * width, width, 1)
        grad_theirs = lax.dynamic_slice_in_dim(grad_attn, (1 - side) * width, width, 1)
        far_positions = flip(positions, "ctx", far_mask)
        slopes_mine = lax.dynamic_slice_in_dim(slopes, side * heads, heads, 0)

    with jax.named_scope("gather_weight"):
        part = qkv_weight.reshape(shard, 3, 2, pairs, PAIR).transpose(0, 2, 3, 1, 4).reshape(shard, 6 * width)
        stacked = ordered(part[None], flip(part, "ctx", far_mask)[None], side)[:, None]
        for position in reversed(range(bits)):
            stacked = widen(stacked, position)
        weight_all = stacked.reshape(model, 6 * width)
        weight, weight_other = by_side(weight_all)

    with jax.named_scope("log_distance"):
        pos = jnp.concatenate([positions, far_positions], 0)
        logd = jnp.log(jnp.abs(pos[:, None] - pos[None, :]).astype(F32) + 1.0) * LOG2E

    with jax.named_scope("exchange_inputs"):
        token_half = lax.dynamic_slice_in_dim(tokens, head_side * half_rows, half_rows, 0)
        piece = half_rows // 3
        near, cross = [], []
        for number in range(3):
            source = token_half[number * piece : (number + 1) * piece]
            if number:
                source = after(source, near[-1], *([logd] if number == 2 else []))
            arrived = flip(source, "ctx", far_mask)
            near.append(arrived)
            cross.append(flip(arrived, "head", 1))
        grad_far = [flip(after(grad_theirs[:, :PAIR], near[1]), "ctx", far_mask)]
        far_tokens = ordered(jnp.concatenate(near, 0), jnp.concatenate(cross, 0), head_side)

    with jax.named_scope("project"):
        qkv_own = jnp.dot(tokens, weight, preferred_element_type=F32).astype(BF16)
        qkv_far = jnp.dot(far_tokens, weight, preferred_element_type=F32).astype(BF16)
        qkv = jnp.concatenate([qkv_own, qkv_far], 0)
        both_tokens = jnp.concatenate([tokens, far_tokens], 0)

    with jax.named_scope("exchange_inputs"):
        late_grad, _ = lax.optimization_barrier((grad_theirs[:, PAIR:], qkv_own))
        grad_far += [flip(late_grad[:, p * PAIR : (p + 1) * PAIR], "ctx", far_mask) for p in range(pairs - 1)]

    with jax.named_scope("gather_other_weight"):
        core = bit_of(0)
        core_half = lax.dynamic_slice_in_dim(weight_all, core * (model // 2), model // 2, 0)
        core_half = after(core_half, qkv_own)
        across_first = flip(core_half[: model // 4], "head", 1)

    tiles = rows // TILE

    def attend(pair, start, stop, grad, sums, dqs, deps, parts=0):
        with jax.named_scope("attention"):
            return attention(pair, start, stop, slopes_mine, qkv, grad, logd, sums, dqs, deps, parts)

    wholes, others, across_own, across_other = [], [], [], []
    before_far, before_own = [], grad_far[1:] + [across_first]
    for pair in range(pairs):
        last = pair == pairs - 1
        cut = slice(pair * PAIR, (pair + 1) * PAIR)
        far_dq, *sums = attend(pair, tiles, 2 * tiles, grad_far[pair], [], [], before_far)
        with jax.named_scope("return_grads"):
            other_dq = flip(far_dq, "ctx", far_mask)
        if not pair:
            with jax.named_scope("gather_other_weight"):
                across_second = flip(after(core_half[model // 4 :], far_dq), "head", 1)
        if pair:
            with jax.named_scope("return_grads"):
                across_other[-1] = flip(after(others[-1], far_dq), "head", 1)
            before_own = [others[-1], across_own[-1], across_second]
        parts = 2 if last else 1
        dqs, begin = [far_dq], 0
        if last:
            begin = tiles - 1
            own_dq, *sums = attend(pair, 0, begin, grad_mine[: begin * TILE, cut], sums, [], before_own)
            dqs.append(own_dq)
            before_own = [across_other[-1], other_dq]
        whole, *far_rest = attend(pair, begin, tiles, grad_mine[begin * TILE :, cut], sums, dqs, before_own, parts)
        before_far = [other_dq]
        with jax.named_scope("return_grads"):
            size = rows // parts
            rest = [flip(f, "ctx", far_mask) for f in far_rest]
            others.append(None if last else jnp.concatenate([other_dq, rest[0]], 1))
            across_own.append(flip(whole[:rows], "head", 1))
        wholes.append(whole)
        across_other.append(None)

    with jax.named_scope("gather_other_weight"):
        across_half = jnp.concatenate([across_first, across_second], 0)
        across_rest = flip(after(across_half, wholes[-1]), "ctx", 1)

    with jax.named_scope("weight_grad"):
        total = lax.dot_general(
            both_tokens, jnp.concatenate(wholes, 1), (((0,), (0,)), ((), ())), preferred_element_type=F32
        ).reshape(2, far_mask // 2, 2, shard, 3 * width)
        total = lax.dynamic_index_in_dim(total, core, 2, keepdims=False) + flip(
            lax.dynamic_index_in_dim(total, 1 - core, 2, keepdims=False), "ctx", 1
        )
        group = (me % far_mask) // 2
        pieces = [lax.dynamic_index_in_dim(total, group, 1, keepdims=False)]
        sends = [
            lax.dynamic_index_in_dim(total, jnp.bitwise_xor(group, apart), 1, keepdims=False)
            for apart in range(1, far_mask // 2)
        ]
        pieces += [flip(send, "ctx", 2 * (n + 1)) for n, send in enumerate(sends)]
        total = sum(pieces[1:], pieces[0])

    with jax.named_scope("return_grads"):
        rest = [after(arrived, *sends) for arrived in rest]
        other = [jnp.concatenate([other_dq[n * size : (n + 1) * size], r], 1) for n, r in enumerate(rest)]
        others[-1] = jnp.concatenate(other, 0)
        across_other[-1] = jnp.concatenate([flip(o, "head", 1) for o in other], 0)

    with jax.named_scope("token_grad"):
        across_all = ordered(across_half, across_rest, core)
        across_weight, across_weight_other = by_side(across_all)

        def product(pieces):
            left = jnp.concatenate([p for p, _ in pieces], 1)
            right = jnp.concatenate([w for _, w in pieces], 1)
            return lax.dot_general(left, right, (((1,), (1,)), ((), ())), preferred_element_type=F32)

        rows_sum = None
        for pair in range(pairs):
            cut = slice(pair * 3 * PAIR, (pair + 1) * 3 * PAIR)
            early = [(wholes[pair][:rows], weight[:, cut]), (across_own[pair], across_weight[:, cut])]
            late = [(others[pair], weight_other[:, cut]), (across_other[pair], across_weight_other[:, cut])]
            if pair < pairs - 1:
                early = early + late
            term = product(early)
            rows_sum = term if rows_sum is None else rows_sum + term
        d_tokens = (rows_sum + product(late)).astype(BF16)

    with jax.named_scope("weight_grad"):
        total = after(total, rows_sum)
        kept = lax.dynamic_index_in_dim(total, side, 0, keepdims=False)
        arrived = flip(lax.dynamic_index_in_dim(total, 1 - side, 0, keepdims=False), "ctx", far_mask)
        d_weight = assemble(side, kept, arrived, d_tokens)
    return (d_tokens, d_weight)


def solution(mesh):
    placed = (P("ctx", None), P("ctx", None, "head"), P("ctx", "head"), P("ctx"), P("head"))
    return jax.shard_map(
        on_device,
        mesh=mesh,
        in_specs=placed,
        out_specs=(P("ctx", None), P("ctx", None, "head")),
        check_vma=False,
    )
```
